512 devices in a mesh: row: 8 (over y), col: 16 (over x_lo, z), layer: 4 (over x_hi, core).
Axes of the slice: x: 4 (x_hi: 2, x_lo: 2; x = x_hi * 2 + x_lo), y: 8, z: 8, core: 2. Of those that a mesh axis runs over, the one named last changes fastest.
Arguments:
- integrals: bfloat16 [64, 1024, 3072], P('layer', 'col', 'row'), may hold values from -0.0234375 to 0.0234375
- amplitudes: bfloat16 [64, 1024, 2048], P('layer', 'row', 'col'), may hold values from -6 to 6
- coulomb: bfloat16 [3072, 2048], P(('row', 'layer'), 'col'), may hold values from -6 to 6
- row_gap: float32 [3072], P(('row', 'layer')), may hold values from 0.5 to 4
- col_gap: float32 [2048], P('col'), may hold values from 0.5 to 4
Outputs:
- residual: float32 [3072, 2048], P(('row', 'layer'), 'col')
The draws below stay inside these ranges and needn't reach their ends.
All inputs are finite; a program needn't handle non-finite values.
Results may differ from the reference program's by a relative error of at most 0.0003.
Values may be sent and summed in bfloat16 or wider, within the bound.
No kernel may reach another device: no remote copies, remote signals or barrier semaphores. Data moves between devices by JAX's collectives and lax.ppermute only.
A program may use at most 64 MiB of HBM per device.

```python
import math
import jax
import jax.numpy as jnp

OCC = 64
VIR = 1024
NROW = 3072
NCOL = 2048


def levels(own_key, shape, split, low, top_value):
    def one(dim, blocks):
        heights = jax.random.uniform(jax.random.fold_in(jax.random.fold_in(own_key, 6), dim), (blocks,), jnp.float32, low / len(split), top_value / len(split))
        return jnp.repeat(jnp.exp(heights), shape[dim] // blocks).reshape((-1,) + (1,) * (len(shape) - dim - 1))

    gain = one(*split[0])
    for cut in split[1:]:
        gain = gain * one(*cut)
    return gain


def scatter_about(key, dims, deviation, bound, cuts=(), dtype=jnp.bfloat16):
    factor_of = levels(key, dims, cuts, -0.22, 0.18) if cuts else 1.0
    entries = jax.random.normal(key, dims, jnp.float32) * deviation * factor_of
    return jnp.minimum(jnp.maximum(entries, -bound), bound).astype(dtype)


def setup_inputs(seed: int = 0) -> dict:
    key_of = jax.random.split(jax.random.key(seed), 6)
    return {
        "integrals": scatter_about(key_of[0], (OCC, VIR, NROW), (OCC * VIR) ** -0.5, 0.0234375, ((0, 4), (1, 16), (2, 8))),
        "amplitudes": scatter_about(key_of[1], (OCC, VIR, NCOL), 1.0, 6.0, ((0, 4), (1, 8), (2, 16))),
        "coulomb": scatter_about(key_of[2], (NROW, NCOL), 1.0, 6.0, ((0, 32), (1, 16))),
        "row_gap": jnp.clip(jnp.exp(math.log(4.0) - 2.0794415 * jax.random.uniform(key_of[3], (NROW,), jnp.float32) ** levels(key_of[3], (NROW,), ((0, 32),), -0.2, 0.2)), 0.5, 4.0),
        "col_gap": jnp.clip(jnp.exp(math.log(4.0) - 2.0794415 * jax.random.uniform(key_of[4], (NCOL,), jnp.float32) ** levels(key_of[4], (NCOL,), ((0, 16),), -0.2, 0.2)), 0.5, 4.0),
    }


def reference(integrals, amplitudes, coulomb, row_gap, col_gap):
    left_matrix = integrals.reshape(OCC * VIR, NROW)
    right_matrix = amplitudes.reshape(OCC * VIR, NCOL)
    product = jnp.dot(left_matrix.T, right_matrix, preferred_element_type=jnp.float32)
    gap_sum = row_gap[:, None] + col_gap[None, :]
    return (coulomb.astype(jnp.float32) + product) / gap_sum
```

```python
import jax
import jax.numpy as jnp
from jax import lax
from jax.sharding import Mesh, PartitionSpec as P

NZ = 8
CONTRACT = (((0, 1, 2), (0, 1, 2)), ((), ()))


def local(integrals, amplitudes, coulomb, row_gap, col_gap):
    z = lax.axis_index("z")
    amp = lax.all_to_all(amplitudes.reshape(2, 8, 128, 128), "xl", 0, 0, tiled=True)
    mine = lax.all_to_all(integrals.reshape(2, 8, 64, 384), "xl", 0, 0, tiled=True)
    amps = lax.all_gather(amp, "y").reshape(2, 4, 2, 8, 2, 64, 128)

    def times(block, source):
        part = lax.dynamic_slice(
            amps, (0, source // 2, 0, 0, source % 2, 0, 0), (2, 1, 2, 8, 1, 64, 128)
        ).reshape(2, 2, 8, 64, 128)
        return [
            lax.dot_general(block, part[:, n], CONTRACT, preferred_element_type=jnp.float32)
            for n in range(2)
        ]

    up = [(i, (i + 1) % NZ) for i in range(NZ)]
    down = [(i, (i - 1) % NZ) for i in range(NZ)]
    total = times(mine, z)
    above = below = mine
    for step in range(1, 4):
        below = lax.ppermute(below, "z", up)
        above = lax.ppermute(above, "z", down)
        for block, source in ((below, (z - step) % NZ), (above, (z + step) % NZ)):
            total = [t + p for t, p in zip(total, times(block, source))]
    last = jnp.concatenate(
        [lax.ppermute(below[:1], "z", up), lax.ppermute(above[1:], "z", down)]
    )
    total = [t + p for t, p in zip(total, times(last, (z + 4) % NZ))]

    shares = jnp.stack(total).reshape(8, 96, 128)
    shares = lax.all_to_all(shares, ("xl", "xh", "core"), 0, 0, tiled=True)
    own = jnp.sum(shares, axis=0)
    gap_sum = row_gap[:, None] + col_gap[None, :]
    return (coulomb.astype(jnp.float32) + own) / gap_sum


def solution(mesh):
    fine = Mesh(mesh.devices.reshape(8, 2, 8, 2, 2), ("y", "xl", "z", "xh", "core"))
    layer, col = ("xh", "core"), ("xl", "z")
    placed = (
        P(layer, col, "y"),
        P(layer, "y", col),
        P(("y",) + layer, col),
        P(("y",) + layer),
        P(col),
    )
    return jax.shard_map(
        local, mesh=fine, in_specs=placed, out_specs=P(("y",) + layer, col), check_vma=False
    )
```

```python
import jax
import jax.numpy as jnp
from jax import lax
from jax.experimental import pallas as pl
from jax.experimental.pallas import tpu as pltpu
from jax.sharding import Mesh, PartitionSpec as P

UP = [(i, (i + 1) % 8) for i in range(8)]
DOWN = [(i, (i - 1) % 8) for i in range(8)]
SWAP = [(0, 1), (1, 0)]
VMEM = pl.BlockSpec(memory_space=pltpu.VMEM)
HBM = pl.BlockSpec(memory_space=pltpu.HBM)
SMEM = pl.BlockSpec(memory_space=pltpu.SMEM)
FLOAT = jnp.float32


def piece(amp_ref, chunk, block):
    y = chunk // 2
    rows = pl.ds(pl.multiple_of((chunk % 2) * 64, 64), 64)
    amp = jnp.concatenate(
        [amp_ref[y, n, :, rows, :].reshape(512, 128) for n in range(2)], axis=1
    )
    return lax.dot_general(
        amp, block.reshape(512, 384), (((0,), (0,)), ((), ())), preferred_element_type=FLOAT
    )


def early_kernel(place, *refs):
    amps, blocks, (amp, out, held, sems) = refs[:8], refs[8:15], refs[15:]
    x, y, z = place[0], place[1], place[2]
    copies = [
        pltpu.make_async_copy(ref, amp.at[lax.rem(y + j, 8)], sems.at[j])
        for j, ref in enumerate(amps)
    ] + [
        pltpu.make_async_copy(ref, held.at[j], sems.at[8 + j]) for j, ref in enumerate(blocks)
    ]
    for copy in copies:
        copy.start()
    for copy in copies[:8]:
        copy.wait()
    total = None
    for j, shift in enumerate((0, 1, 2, 3, -1, -2, -3)):
        copies[8 + j].wait()
        source = lax.rem(z + shift + 8, 8)
        for half in range(2):
            part = piece(amp, lax.rem(x + half, 2) * 8 + source, held[j, half])
            total = part if total is None else total + part
    out[...] = total


def late_kernel(place, early, amp, last_own, last_other, out):
    x, z = place[0], place[2]
    source = lax.rem(z + 4, 8)
    total = early[...]
    for half, ref in enumerate((last_own, last_other)):
        total = total + piece(amp, lax.rem(x + half, 2) * 8 + source, ref[...])
    for n in range(2):
        out[lax.rem(x + n, 2)] = total[n * 128 : (n + 1) * 128].T


def local(integrals, amplitudes, coulomb, row_gap, col_gap):
    x, y, z = (lax.axis_index(a) for a in ("xl", "y", "z"))
    place = jnp.stack([x, y, z])

    def swap(block):
        keep = lax.dynamic_slice_in_dim(block, x * 8, 8, 0)
        give = lax.dynamic_slice_in_dim(block, (1 - x) * 8, 8, 0)
        return jnp.stack([keep, lax.ppermute(give, "xl", SWAP)])

    def ring(own, axis):
        above, below = [own], [own]
        for _ in range(3):
            below.append(lax.ppermute(below[-1], axis, UP))
            above.append(lax.ppermute(above[-1], axis, DOWN))
        far = lax.ppermute(below[3][0], axis, UP), lax.ppermute(above[3][1], axis, DOWN)
        return above, below, far

    above, below, far = ring(swap(integrals), "z")
    a_above, a_below, a_far = ring(swap(amplitudes), "y")
    amps = a_above + [jnp.stack(a_far)] + a_below[:0:-1]
    early, amp = pl.pallas_call(
        early_kernel,
        out_shape=(
            jax.ShapeDtypeStruct((8, 2, 8, 128, 128), jnp.bfloat16),
            jax.ShapeDtypeStruct((256, 384), FLOAT),
        ),
        in_specs=[SMEM] + [HBM] * 15,
        out_specs=(VMEM, VMEM),
        scratch_shapes=[
            pltpu.VMEM((7, 2, 8, 64, 384), jnp.bfloat16),
            pltpu.SemaphoreType.DMA((15,)),
        ],
        compiler_params=pltpu.CompilerParams(vmem_limit_bytes=24 << 20),
        cost_estimate=pl.CostEstimate(flops=1 << 30, bytes_accessed=16 << 20, transcendentals=0),
    )(place, *amps, *above, *below[1:])[::-1]
    shares = pl.pallas_call(
        late_kernel,
        out_shape=jax.ShapeDtypeStruct((2, 384, 128), FLOAT),
        in_specs=[SMEM] + [VMEM] * 4,
        out_specs=VMEM,
        compiler_params=pltpu.CompilerParams(vmem_limit_bytes=6 << 20),
    )(place, early, amp, *far)
    shares = lax.all_to_all(
        shares.reshape(8, 96, 128), ("xl", "xh", "core"), 0, 0, tiled=True
    )
    own = jnp.sum(shares, axis=0)
    gap_sum = row_gap[:, None] + col_gap[None, :]
    return (coulomb.astype(FLOAT) + own) / gap_sum


def solution(mesh):
    fine = Mesh(mesh.devices.reshape(8, 2, 8, 2, 2), ("y", "xl", "z", "xh", "core"))
    layer, col = ("xh", "core"), ("xl", "z")
    placed = (
        P(layer, col, "y"),
        P(layer, "y", col),
        P(("y",) + layer, col),
        P(("y",) + layer),
        P(col),
    )
    return jax.shard_map(
        local, mesh=fine, in_specs=placed, out_specs=P(("y",) + layer, col), check_vma=False
    )
```

```python
import jax
import jax.numpy as jnp
from jax import lax
from jax.experimental import pallas as pl
from jax.experimental.pallas import tpu as pltpu
from jax.sharding import Mesh, PartitionSpec as P

FORTH = [(2 * i + c, 2 * ((i + 1 - 2 * c) % 8) + c) for i in range(8) for c in range(2)]
BACK = [(j, i) for i, j in FORTH]
SWAP = [(0, 1), (1, 0)]
VMEM = pl.BlockSpec(memory_space=pltpu.VMEM)
ANY = pl.BlockSpec(memory_space=pl.ANY)
SMEM = pl.BlockSpec(memory_space=pltpu.SMEM)
FLOAT = jnp.float32


def piece(amp_ref, chunk, block):
    y = chunk // 2
    rows = pl.ds(pl.multiple_of((chunk % 2) * 64, 64), 64)
    amp = jnp.concatenate(
        [amp_ref[y, n, :, rows, :].reshape(512, 128) for n in range(2)], axis=1
    )
    return lax.dot_general(
        amp, block.reshape(512, 384), (((0,), (0,)), ((), ())), preferred_element_type=FLOAT
    )


def early_kernel(place, *refs):
    amps, blocks, (amp, out, held, sems) = refs[:8], refs[8:15], refs[15:]
    x, y, z, way = place[0], place[1], place[2], place[3]
    copies = [
        pltpu.make_async_copy(ref, amp.at[lax.rem(y + way * shift + 8, 8)], sems.at[j])
        for j, (ref, shift) in enumerate(zip(amps, (0, -1, -2, -3, -4, 1, 2, 3)))
    ] + [
        pltpu.make_async_copy(ref, held.at[j], sems.at[8 + j]) for j, ref in enumerate(blocks)
    ]
    for copy in copies:
        copy.start()
    for copy in copies[:8]:
        copy.wait()
    total = None
    for j, shift in enumerate((0, -1, -2, -3, 1, 2, 3)):
        copies[8 + j].wait()
        source = lax.rem(z + way * shift + 8, 8)
        for half in range(2):
            part = piece(amp, lax.rem(x + half, 2) * 8 + source, held[j, half])
            total = part if total is None else total + part
    out[...] = total


def late_kernel(place, early, amp, last, out):
    x, z = place[0], place[2]
    source = lax.rem(z + 4, 8)
    total = early[...]
    for half in range(2):
        total = total + piece(amp, lax.rem(x + half, 2) * 8 + source, last[half])
    for n in range(2):
        out[lax.rem(x + n, 2)] = total[n * 128 : (n + 1) * 128].T


def local(integrals, amplitudes, coulomb, row_gap, col_gap):
    place = [lax.axis_index(a) for a in ("xl", "y", "z")] + [1 - 2 * lax.axis_index("core")]
    place = lax.optimization_barrier(jnp.stack(place))
    x = place[0]

    def swap(block):
        keep = lax.dynamic_slice_in_dim(block, x * 8, 8, 0)
        give = lax.dynamic_slice_in_dim(block, (1 - x) * 8, 8, 0)
        return jnp.stack([keep, lax.ppermute(give, "xl", SWAP)])

    def ring(own, axis):
        forth, back = [own], [own]
        for _ in range(3):
            forth.append(lax.ppermute(forth[-1], (axis, "core"), FORTH))
            back.append(lax.ppermute(back[-1], (axis, "core"), BACK))
        return forth + [lax.ppermute(forth[3], (axis, "core"), FORTH)] + back[1:]

    blocks = ring(swap(integrals), "z")
    amps = ring(swap(amplitudes), "y")
    early, amp = pl.pallas_call(
        early_kernel,
        out_shape=(
            jax.ShapeDtypeStruct((8, 2, 8, 128, 128), jnp.bfloat16),
            jax.ShapeDtypeStruct((256, 384), FLOAT),
        ),
        in_specs=[SMEM] + [ANY] * 15,
        out_specs=(VMEM, VMEM),
        scratch_shapes=[
            pltpu.VMEM((7, 2, 8, 64, 384), jnp.bfloat16),
            pltpu.SemaphoreType.DMA((15,)),
        ],
        compiler_params=pltpu.CompilerParams(vmem_limit_bytes=24 << 20),
        cost_estimate=pl.CostEstimate(flops=1 << 30, bytes_accessed=16 << 20, transcendentals=0),
    )(place, *amps, *blocks[:4], *blocks[5:])[::-1]
    shares = pl.pallas_call(
        late_kernel,
        out_shape=jax.ShapeDtypeStruct((2, 384, 128), FLOAT),
        in_specs=[SMEM] + [VMEM] * 3,
        out_specs=VMEM,
        compiler_params=pltpu.CompilerParams(vmem_limit_bytes=6 << 20),
    )(place, early, amp, blocks[4])
    shares = lax.all_to_all(
        shares.reshape(8, 96, 128), ("xl", "xh", "core"), 0, 0, tiled=True
    )
    own = jnp.sum(shares, axis=0)
    gap_sum = row_gap[:, None] + col_gap[None, :]
    return (coulomb.astype(FLOAT) + own) / gap_sum


def solution(mesh):
    fine = Mesh(mesh.devices.reshape(8, 2, 8, 2, 2), ("y", "xl", "z", "xh", "core"))
    layer, col = ("xh", "core"), ("xl", "z")
    placed = (
        P(layer, col, "y"),
        P(layer, "y", col),
        P(("y",) + layer, col),
        P(("y",) + layer),
        P(col),
    )
    return jax.shard_map(
        local, mesh=fine, in_specs=placed, out_specs=P(("y",) + layer, col), check_vma=False
    )
```

```python
import jax
import jax.numpy as jnp
from jax import lax
from jax.experimental import pallas as pl
from jax.experimental.pallas import tpu as pltpu
from jax.sharding import Mesh, PartitionSpec as P

UP = [(i, (i + 1) % 8) for i in range(8)]
DOWN = [(i, (i - 1) % 8) for i in range(8)]
TRADE = [
    (2 * y + x, 2 * y + x if y // 4 == x else 2 * (7 - y) + 1 - x) for y in range(8) for x in range(2)
]
SHIFTS = (0, -1, -2, -3, 1, 2, 3)
ANY = pl.BlockSpec(memory_space=pl.ANY)
SMEM = pl.BlockSpec(memory_space=pltpu.SMEM)
VMEM = pl.BlockSpec(memory_space=pltpu.VMEM)
FLOAT = jnp.float32


def piece(place, amp_ref, source, block, first):
    y = place[0] * 4 + source // 2
    rows = pl.ds(pl.multiple_of(lax.rem(source, 2) * 64, 64), 64)
    count = block.shape[0]
    amp = jnp.concatenate(
        [
            amp_ref[slot, first : first + count, rows, :].reshape(count * 64, 128)
            for slot in (y, 7 - y)
        ],
        axis=1,
    )
    return lax.dot_general(
        amp,
        block.reshape(count * 64, 384),
        (((0,), (0,)), ((), ())),
        preferred_element_type=FLOAT,
    )


def early_kernel(place, *refs):
    amps, far, blocks, (amp, out, held, sems) = refs[:7], refs[7:9], refs[9:16], refs[16:]
    y, z = place[1], place[2]
    targets = [amp.at[lax.rem(y + shift + 8, 8)] for shift in SHIFTS]
    opposite = amp.at[lax.rem(y + 4, 8)]
    targets += [opposite.at[pl.ds(0, 8)], opposite.at[pl.ds(8, 8)]]
    targets += [held.at[j] for j in range(7)]
    copies = [
        pltpu.make_async_copy(ref, target, sems.at[j])
        for j, (ref, target) in enumerate(zip(amps + far + blocks, targets))
    ]
    for copy in copies:
        copy.start()
    for copy in copies[:9]:
        copy.wait()
    total = None
    for j, shift in enumerate(SHIFTS):
        copies[9 + j].wait()
        part = piece(place, amp, lax.rem(z + shift + 8, 8), held[j], 0)
        total = part if total is None else total + part
    out[...] = total


def late_kernel(place, early, amp, far_low, far_high, out):
    source = lax.rem(place[2] + 4, 8)
    total = early[...]
    for first, far in ((0, far_low), (8, far_high)):
        total = total + piece(place, amp, source, far[...], first)
    for n in range(2):
        out[lax.rem(place[0] + n, 2)] = total[n * 128 : (n + 1) * 128].T


def ring(own, axis):
    below, above = [own], [own]
    for _ in range(3):
        below.append(lax.ppermute(below[-1], axis, UP))
        above.append(lax.ppermute(above[-1], axis, DOWN))
    far = [lax.ppermute(below[3][:8], axis, UP), lax.ppermute(above[3][8:], axis, DOWN)]
    return below + above[1:], far


def local(integrals, amplitudes, coulomb, row_gap, col_gap):
    place = jnp.stack([lax.axis_index(a) for a in ("xl", "y", "z")])
    place, integrals, amplitudes = lax.optimization_barrier((place, integrals, amplitudes))
    blocks, far = ring(integrals, "z")
    amps, a_far = ring(lax.ppermute(amplitudes, ("y", "xl"), TRADE), "y")
    early, amp = pl.pallas_call(
        early_kernel,
        out_shape=(
            jax.ShapeDtypeStruct((8, 16, 128, 128), jnp.bfloat16),
            jax.ShapeDtypeStruct((256, 384), FLOAT),
        ),
        in_specs=[SMEM] + [ANY] * 16,
        out_specs=(VMEM, VMEM),
        scratch_shapes=[
            pltpu.VMEM((7, 16, 64, 384), jnp.bfloat16),
            pltpu.SemaphoreType.DMA((16,)),
        ],
        compiler_params=pltpu.CompilerParams(vmem_limit_bytes=24 << 20),
        cost_estimate=pl.CostEstimate(flops=1 << 30, bytes_accessed=16 << 20, transcendentals=0),
    )(place, *amps, *a_far, *blocks)[::-1]
    shares = pl.pallas_call(
        late_kernel,
        out_shape=jax.ShapeDtypeStruct((2, 384, 128), FLOAT),
        in_specs=[SMEM] + [VMEM] * 4,
        out_specs=VMEM,
        compiler_params=pltpu.CompilerParams(vmem_limit_bytes=6 << 20),
    )(place, early, amp, *far)
    shares = lax.all_to_all(
        shares.reshape(8, 96, 128), ("xl", "xh", "core"), 0, 0, tiled=True
    )
    own = jnp.sum(shares, axis=0)
    gap_sum = row_gap[:, None] + col_gap[None, :]
    return (coulomb.astype(FLOAT) + own) / gap_sum


def solution(mesh):
    fine = Mesh(mesh.devices.reshape(8, 2, 8, 2, 2), ("y", "xl", "z", "xh", "core"))
    layer, col = ("xh", "core"), ("xl", "z")
    placed = (
        P(layer, col, "y"),
        P(layer, "y", col),
        P(("y",) + layer, col),
        P(("y",) + layer),
        P(col),
    )
    return jax.shard_map(
        local, mesh=fine, in_specs=placed, out_specs=P(("y",) + layer, col), check_vma=False
    )
```

```python
import jax
import jax.numpy as jnp
from jax import lax
from jax.experimental import pallas as pl
from jax.experimental.pallas import tpu as pltpu
from jax.sharding import Mesh, PartitionSpec as P

UP = [(i, (i + 1) % 8) for i in range(8)]
DOWN = [(i, (i - 1) % 8) for i in range(8)]
TRADE = [
    (2 * y + x, 2 * y + x if y // 4 == x else 2 * (7 - y) + 1 - x) for y in range(8) for x in range(2)
]
SHIFTS = (0, -1, -2, -3, 1, 2, 3)
ANY = pl.BlockSpec(memory_space=pl.ANY)
SMEM = pl.BlockSpec(memory_space=pltpu.SMEM)
VMEM = pl.BlockSpec(memory_space=pltpu.VMEM)
FLOAT = jnp.float32


def columns(amp_ref, slot, source):
    rows = pl.ds(pl.multiple_of(lax.rem(source, 2) * 64, 64), 64)
    return amp_ref[slot, :, rows, :].reshape(1024, 128)


def times(amp, block):
    return lax.dot_general(
        amp, block.reshape(1024, 384), (((0,), (0,)), ((), ())), preferred_element_type=FLOAT
    )


def piece(x, amp_ref, source, block):
    y = x * 4 + source // 2
    return times(
        jnp.concatenate([columns(amp_ref, slot, source) for slot in (y, 7 - y)], axis=1), block
    )


def early_kernel(place, *refs):
    (amps, blocks), (amp, held, out, sems) = (refs[:7], refs[7:14]), refs[14:]
    x, y, z = place[0], place[1], place[2]
    turns = [lax.rem(shift + 8, 8) for shift in SHIFTS]
    copies = [
        pltpu.make_async_copy(ref, amp.at[lax.rem(y + turn, 8)], sems.at[j])
        for j, (ref, turn) in enumerate(zip(amps, turns))
    ] + [
        pltpu.make_async_copy(ref, held.at[lax.rem(z + turn, 8)], sems.at[7 + j])
        for j, (ref, turn) in enumerate(zip(blocks, turns))
    ]
    for copy in copies:
        copy.start()
    amp[lax.rem(y + 4, 8)] = jnp.zeros((16, 128, 128), jnp.bfloat16)
    for copy in copies[:7]:
        copy.wait()
    total = None
    for j, turn in enumerate(turns):
        copies[7 + j].wait()
        source = lax.rem(z + turn, 8)
        part = piece(x, amp, source, held[source])
        total = part if total is None else total + part
    out[...] = total


def late_kernel(place, early, amp_in, held, amp_far, block_far, out, total):
    x, y, z = place[0], place[1], place[2]
    slot, opposite = lax.rem(y + 4, 8), lax.rem(z + 4, 8)
    mine = x * 4 + opposite // 2
    pair = jnp.concatenate(
        [
            jnp.where(at == slot, columns(amp_far, 0, opposite), columns(amp_in, at, opposite))
            for at in (mine, 7 - mine)
        ],
        axis=1,
    )
    total[...] = early[...] + times(pair, block_far[...])
    other = jnp.where(slot // 4 == x, 0, 1)
    first = lax.rem(jnp.where(other == 0, slot, 7 - slot), 4) * 2
    for source in (first, first + 1):

        @pl.when(source != opposite)
        def _():
            at = pl.ds(pl.multiple_of(other * 128, 128), 128)
            total[at, :] += times(columns(amp_far, 0, source), held[source])

    for n in range(2):
        out[lax.rem(x + n, 2)] = total[n * 128 : (n + 1) * 128].T


def after(block, *arrived):
    return lax.optimization_barrier((block,) + arrived)[0]


def local(integrals, amplitudes, coulomb, row_gap, col_gap):
    place = jnp.stack([lax.axis_index(a) for a in ("xl", "y", "z")])
    place, integrals, amplitudes = lax.optimization_barrier((place, integrals, amplitudes))

    def up(block, axis, *arrived):
        return lax.ppermute(after(block, *arrived), axis, UP)

    def down(block, axis, *arrived):
        return lax.ppermute(after(block, *arrived), axis, DOWN)

    a0 = lax.ppermute(amplitudes, ("y", "xl"), TRADE)
    i0 = integrals
    iu1, id1 = up(i0, "z"), down(i0, "z")
    iu2 = up(iu1, "z")
    au1, ad1 = up(a0, "y", iu1), down(a0, "y", iu1)
    id2 = down(id1, "z", a0)
    au2 = up(au1, "y", id1)
    iu3 = up(iu2, "z", au1)
    ad2 = down(ad1, "y", iu2)
    au3 = up(au2, "y", ad1)
    id3 = down(id2, "z", au2)
    iu4 = up(iu3, "z", id2)
    ad3 = down(ad2, "y", iu3)
    au4 = up(au3, "y", ad2)
    held_shape = jax.ShapeDtypeStruct((8, 16, 64, 384), jnp.bfloat16)
    amp_shape = jax.ShapeDtypeStruct((8, 16, 128, 128), jnp.bfloat16)
    amp, held, early = pl.pallas_call(
        early_kernel,
        out_shape=(amp_shape, held_shape, jax.ShapeDtypeStruct((256, 384), FLOAT)),
        in_specs=[SMEM] + [ANY] * 14,
        out_specs=(VMEM, VMEM, VMEM),
        scratch_shapes=[pltpu.SemaphoreType.DMA((14,))],
        compiler_params=pltpu.CompilerParams(vmem_limit_bytes=24 << 20),
        cost_estimate=pl.CostEstimate(flops=1 << 30, bytes_accessed=16 << 20, transcendentals=0),
    )(place, a0, au1, au2, au3, ad1, ad2, ad3, i0, iu1, iu2, iu3, id1, id2, id3)
    shares = pl.pallas_call(
        late_kernel,
        out_shape=jax.ShapeDtypeStruct((2, 384, 128), FLOAT),
        in_specs=[SMEM] + [VMEM] * 5,
        out_specs=VMEM,
        scratch_shapes=[pltpu.VMEM((256, 384), FLOAT)],
        compiler_params=pltpu.CompilerParams(vmem_limit_bytes=8 << 20),
    )(place, early, amp, held, au4[None], iu4)
    shares = lax.all_to_all(
        shares.reshape(8, 96, 128), ("xl", "xh", "core"), 0, 0, tiled=True
    )
    own = jnp.sum(shares, axis=0)
    gap_sum = row_gap[:, None] + col_gap[None, :]
    return (coulomb.astype(FLOAT) + own) / gap_sum


def solution(mesh):
    fine = Mesh(mesh.devices.reshape(8, 2, 8, 2, 2), ("y", "xl", "z", "xh", "core"))
    layer, col = ("xh", "core"), ("xl", "z")
    placed = (
        P(layer, col, "y"),
        P(layer, "y", col),
        P(("y",) + layer, col),
        P(("y",) + layer),
        P(col),
    )
    return jax.shard_map(
        local, mesh=fine, in_specs=placed, out_specs=P(("y",) + layer, col), check_vma=False
    )
```

```python
import jax
import jax.numpy as jnp
from jax import lax
from jax.experimental import pallas as pl
from jax.experimental.pallas import tpu as pltpu
from jax.sharding import Mesh, PartitionSpec as P

UP = [(i, (i + 1) % 8) for i in range(8)]
DOWN = [(i, (i - 1) % 8) for i in range(8)]
TRADE = [
    (2 * y + x, 2 * y + x if y // 4 == x else 2 * (7 - y) + 1 - x) for y in range(8) for x in range(2)
]
SHIFTS = (0, -1, -2, -3, 1, 2)
LATE = (3, 4)
ANY = pl.BlockSpec(memory_space=pl.ANY)
SMEM = pl.BlockSpec(memory_space=pltpu.SMEM)
VMEM = pl.BlockSpec(memory_space=pltpu.VMEM)
FLOAT = jnp.float32


def columns(amp_ref, slot, source):
    rows = pl.ds(pl.multiple_of(lax.rem(source, 2) * 64, 64), 64)
    return amp_ref[slot, :, rows, :].reshape(1024, 128)


def times(amp, block):
    return lax.dot_general(
        amp, block.reshape(1024, 384), (((0,), (0,)), ((), ())), preferred_element_type=FLOAT
    )


def piece(x, amp_ref, source, block):
    y = x * 4 + source // 2
    return times(
        jnp.concatenate([columns(amp_ref, slot, source) for slot in (y, 7 - y)], axis=1), block
    )


def early_kernel(place, *refs):
    count = len(SHIFTS)
    amps, blocks, (amp, held, out, sems) = refs[:count], refs[count : 2 * count], refs[2 * count :]
    x, y, z = place[0], place[1], place[2]
    turns = [lax.rem(shift + 8, 8) for shift in SHIFTS]
    copies = [
        pltpu.make_async_copy(ref, amp.at[lax.rem(y + turn, 8)], sems.at[j])
        for j, (ref, turn) in enumerate(zip(amps, turns))
    ] + [
        pltpu.make_async_copy(ref, held.at[lax.rem(z + turn, 8)], sems.at[count + j])
        for j, (ref, turn) in enumerate(zip(blocks, turns))
    ]
    for copy in copies:
        copy.start()
    for turn in LATE:
        amp[lax.rem(y + turn, 8)] = jnp.zeros((16, 128, 128), jnp.bfloat16)
    for copy in copies[:count]:
        copy.wait()
    total = None
    for j, turn in enumerate(turns):
        copies[count + j].wait()
        source = lax.rem(z + turn, 8)
        part = piece(x, amp, source, held[source])
        total = part if total is None else total + part
    out[...] = total


def late_kernel(place, early, amp_in, held, *refs):
    count = len(LATE)
    amps, blocks, (out, total) = refs[:count], refs[count : 2 * count], refs[2 * count :]
    x, y, z = place[0], place[1], place[2]
    slots = [lax.rem(y + turn, 8) for turn in LATE]
    sources = [lax.rem(z + turn, 8) for turn in LATE]

    def either(at, source):
        amp = columns(amp_in, at, source)
        for slot, ref in zip(slots, amps):
            amp = jnp.where(at == slot, columns(ref, 0, source), amp)
        return amp

    new = early[...]
    for source, ref in zip(sources, blocks):
        at = x * 4 + source // 2
        pair = jnp.concatenate([either(at, source), either(7 - at, source)], axis=1)
        new = new + times(pair, ref[...])
    total[...] = new
    for slot, ref in zip(slots, amps):
        other = jnp.where(slot // 4 == x, 0, 1)
        first = lax.rem(jnp.where(other == 0, slot, 7 - slot), 4) * 2
        for source in (first, first + 1):
            fresh = source != sources[0]
            for late in sources[1:]:
                fresh &= source != late

            @pl.when(fresh)
            def _():
                at = pl.ds(pl.multiple_of(other * 128, 128), 128)
                total[at, :] += times(columns(ref, 0, source), held[source])

    for n in range(2):
        out[lax.rem(x + n, 2)] = total[n * 128 : (n + 1) * 128].T


def after(block, *arrived):
    return lax.optimization_barrier((block,) + arrived)[0]


def local(integrals, amplitudes, coulomb, row_gap, col_gap):
    place = jnp.stack([lax.axis_index(a) for a in ("xl", "y", "z")])
    place, integrals, amplitudes = lax.optimization_barrier((place, integrals, amplitudes))

    def up(block, axis, *arrived):
        return lax.ppermute(after(block, *arrived), axis, UP)

    def down(block, axis, *arrived):
        return lax.ppermute(after(block, *arrived), axis, DOWN)

    i0 = integrals
    iu1 = up(i0, "z")
    a0 = lax.ppermute(amplitudes, ("y", "xl"), TRADE)
    id1 = down(i0, "z")
    iu2 = up(iu1, "z")
    au1 = up(a0, "y")
    id2 = down(id1, "z")
    ad1 = down(a0, "y", id1)
    au2 = up(au1, "y")
    iu3 = up(iu2, "z")
    ad2 = down(ad1, "y")
    id3 = down(id2, "z")
    au3 = up(au2, "y")
    iu4 = up(iu3, "z")
    ad3 = down(ad2, "y")
    au4 = up(au3, "y")
    held_shape = jax.ShapeDtypeStruct((8, 16, 64, 384), jnp.bfloat16)
    amp_shape = jax.ShapeDtypeStruct((8, 16, 128, 128), jnp.bfloat16)
    amp, held, early = pl.pallas_call(
        early_kernel,
        out_shape=(amp_shape, held_shape, jax.ShapeDtypeStruct((256, 384), FLOAT)),
        in_specs=[SMEM] + [ANY] * 12,
        out_specs=(VMEM, VMEM, VMEM),
        scratch_shapes=[pltpu.SemaphoreType.DMA((12,))],
        compiler_params=pltpu.CompilerParams(vmem_limit_bytes=24 << 20),
        cost_estimate=pl.CostEstimate(flops=1 << 30, bytes_accessed=16 << 20, transcendentals=0),
    )(place, a0, au1, au2, au3, ad1, ad2, i0, iu1, iu2, iu3, id1, id2)
    shares = pl.pallas_call(
        late_kernel,
        out_shape=jax.ShapeDtypeStruct((2, 384, 128), FLOAT),
        in_specs=[SMEM] + [VMEM] * 7,
        out_specs=VMEM,
        scratch_shapes=[pltpu.VMEM((256, 384), FLOAT)],
        compiler_params=pltpu.CompilerParams(vmem_limit_bytes=8 << 20),
    )(place, early, amp, held, ad3[None], au4[None], id3, iu4)
    shares = lax.all_to_all(
        shares.reshape(8, 96, 128), ("xl", "xh", "core"), 0, 0, tiled=True
    )
    own = jnp.sum(shares, axis=0)
    gap_sum = row_gap[:, None] + col_gap[None, :]
    return (coulomb.astype(FLOAT) + own) / gap_sum


def solution(mesh):
    fine = Mesh(mesh.devices.reshape(8, 2, 8, 2, 2), ("y", "xl", "z", "xh", "core"))
    layer, col = ("xh", "core"), ("xl", "z")
    placed = (
        P(layer, col, "y"),
        P(layer, "y", col),
        P(("y",) + layer, col),
        P(("y",) + layer),
        P(col),
    )
    return jax.shard_map(
        local, mesh=fine, in_specs=placed, out_specs=P(("y",) + layer, col), check_vma=False
    )
```

```python
import jax
import jax.numpy as jnp
from jax import lax
from jax.experimental import pallas as pl
from jax.experimental.pallas import tpu as pltpu
from jax.sharding import Mesh, PartitionSpec as P

FORTH = [(2 * i + c, 2 * ((i + 1 - 2 * c) % 8) + c) for i in range(8) for c in range(2)]
BACK = [(j, i) for i, j in FORTH]
TRADE = [
    (2 * y + x, 2 * y + x if y // 4 == x else 2 * (7 - y) + 1 - x) for y in range(8) for x in range(2)
]
SHIFTS = (0, -1, -2, -3, 1, 2)
LATE = (3, 4)
ANY = pl.BlockSpec(memory_space=pl.ANY)
SMEM = pl.BlockSpec(memory_space=pltpu.SMEM)
VMEM = pl.BlockSpec(memory_space=pltpu.VMEM)
FLOAT = jnp.float32


def columns(amp_ref, slot, source):
    rows = pl.ds(pl.multiple_of(lax.rem(source, 2) * 64, 64), 64)
    return amp_ref[slot, :, rows, :].reshape(1024, 128)


def times(amp, block):
    return lax.dot_general(
        amp, block.reshape(1024, 384), (((0,), (0,)), ((), ())), preferred_element_type=FLOAT
    )


def piece(x, amp_ref, source, block):
    y = x * 4 + source // 2
    return times(
        jnp.concatenate([columns(amp_ref, slot, source) for slot in (y, 7 - y)], axis=1), block
    )


def early_kernel(place, *refs):
    count = len(SHIFTS)
    amps, blocks, (amp, held, out, sems) = refs[:count], refs[count : 2 * count], refs[2 * count :]
    x, y, z, way = place[0], place[1], place[2], 1 - 2 * place[3]
    turns = [lax.rem(way * shift + 8, 8) for shift in SHIFTS]
    copies = [
        pltpu.make_async_copy(ref, amp.at[lax.rem(y + turn, 8)], sems.at[j])
        for j, (ref, turn) in enumerate(zip(amps, turns))
    ] + [
        pltpu.make_async_copy(ref, held.at[lax.rem(z + turn, 8)], sems.at[count + j])
        for j, (ref, turn) in enumerate(zip(blocks, turns))
    ]
    for copy in copies:
        copy.start()
    for turn in LATE:
        amp[lax.rem(y + way * turn + 8, 8)] = jnp.zeros((16, 128, 128), jnp.bfloat16)
    for copy in copies[:count]:
        copy.wait()
    total = None
    for j, turn in enumerate(turns):
        copies[count + j].wait()
        source = lax.rem(z + turn, 8)
        part = piece(x, amp, source, held[source])
        total = part if total is None else total + part
    out[...] = total


def late_kernel(place, early, amp_in, held, *refs):
    count = len(LATE)
    amps, blocks, (out, total) = refs[:count], refs[count : 2 * count], refs[2 * count :]
    x, y, z, way = place[0], place[1], place[2], 1 - 2 * place[3]
    slots = [lax.rem(y + way * turn + 8, 8) for turn in LATE]
    sources = [lax.rem(z + way * turn + 8, 8) for turn in LATE]

    def either(at, source):
        amp = columns(amp_in, at, source)
        for slot, ref in zip(slots, amps):
            amp = jnp.where(at == slot, columns(ref, 0, source), amp)
        return amp

    new = early[...]
    for source, ref in zip(sources, blocks):
        at = x * 4 + source // 2
        pair = jnp.concatenate([either(at, source), either(7 - at, source)], axis=1)
        new = new + times(pair, ref[...])
    total[...] = new
    for slot, ref in zip(slots, amps):
        other = jnp.where(slot // 4 == x, 0, 1)
        first = lax.rem(jnp.where(other == 0, slot, 7 - slot), 4) * 2
        for source in (first, first + 1):
            fresh = source != sources[0]
            for late in sources[1:]:
                fresh &= source != late

            @pl.when(fresh)
            def _():
                at = pl.ds(pl.multiple_of(other * 128, 128), 128)
                total[at, :] += times(columns(ref, 0, source), held[source])

    for n in range(2):
        out[lax.rem(x + n, 2)] = total[n * 128 : (n + 1) * 128].T


def after(block, *arrived):
    return lax.optimization_barrier((block,) + arrived)[0]


def local(integrals, amplitudes, coulomb, row_gap, col_gap):
    place = jnp.stack([lax.axis_index(a) for a in ("xl", "y", "z", "core")])
    place, integrals, amplitudes = lax.optimization_barrier((place, integrals, amplitudes))

    def forth(block, axis, *arrived):
        return lax.ppermute(after(block, *arrived), (axis, "core"), FORTH)

    def back(block, axis, *arrived):
        return lax.ppermute(after(block, *arrived), (axis, "core"), BACK)

    i0 = integrals
    iu1 = forth(i0, "z")
    a0 = lax.ppermute(amplitudes, ("y", "xl"), TRADE)
    id1 = back(i0, "z")
    iu2 = forth(iu1, "z")
    au1 = forth(a0, "y", iu1)
    ad1 = back(a0, "y", iu1)
    id2 = back(id1, "z", a0)
    au2 = forth(au1, "y", id1)
    iu3 = forth(iu2, "z", au1)
    id3 = back(id2, "z", iu2)
    au3 = forth(au2, "y", id2)
    ad2 = back(ad1, "y", au2)
    iu4 = forth(iu3, "z", ad1)
    au4 = forth(au3, "y", iu3)
    ad3 = back(ad2, "y", au3)
    held_shape = jax.ShapeDtypeStruct((8, 16, 64, 384), jnp.bfloat16)
    amp_shape = jax.ShapeDtypeStruct((8, 16, 128, 128), jnp.bfloat16)
    amp, held, early = pl.pallas_call(
        early_kernel,
        out_shape=(amp_shape, held_shape, jax.ShapeDtypeStruct((256, 384), FLOAT)),
        in_specs=[SMEM] + [ANY] * 12,
        out_specs=(VMEM, VMEM, VMEM),
        scratch_shapes=[pltpu.SemaphoreType.DMA((12,))],
        compiler_params=pltpu.CompilerParams(vmem_limit_bytes=24 << 20),
        cost_estimate=pl.CostEstimate(flops=1 << 30, bytes_accessed=16 << 20, transcendentals=0),
    )(place, a0, au1, au2, au3, ad1, ad2, i0, iu1, iu2, iu3, id1, id2)
    shares = pl.pallas_call(
        late_kernel,
        out_shape=jax.ShapeDtypeStruct((2, 384, 128), FLOAT),
        in_specs=[SMEM] + [VMEM] * 7,
        out_specs=VMEM,
        scratch_shapes=[pltpu.VMEM((256, 384), FLOAT)],
        compiler_params=pltpu.CompilerParams(vmem_limit_bytes=8 << 20),
    )(place, early, amp, held, ad3[None], au4[None], id3, iu4)
    shares = lax.all_to_all(
        shares.reshape(8, 96, 128), ("xl", "xh", "core"), 0, 0, tiled=True
    )
    own = jnp.sum(shares, axis=0)
    gap_sum = row_gap[:, None] + col_gap[None, :]
    return (coulomb.astype(FLOAT) + own) / gap_sum


def solution(mesh):
    fine = Mesh(mesh.devices.reshape(8, 2, 8, 2, 2), ("y", "xl", "z", "xh", "core"))
    layer, col = ("xh", "core"), ("xl", "z")
    placed = (
        P(layer, col, "y"),
        P(layer, "y", col),
        P(("y",) + layer, col),
        P(("y",) + layer),
        P(col),
    )
    return jax.shard_map(
        local, mesh=fine, in_specs=placed, out_specs=P(("y",) + layer, col), check_vma=False
    )
```

```python
import jax
import jax.numpy as jnp
from jax import lax
from jax.experimental import pallas as pl
from jax.experimental.pallas import tpu as pltpu
from jax.sharding import Mesh, PartitionSpec as P

FORTH = [(2 * i + c, 2 * ((i + 1 - 2 * c) % 8) + c) for i in range(8) for c in range(2)]
BACK = [(j, i) for i, j in FORTH]
TRADE = [
    (2 * y + x, 2 * y + x if y // 4 == x else 2 * (7 - y) + 1 - x) for y in range(8) for x in range(2)
]
SHIFTS = (0, -1, -2, -3, 1, 2)
LATE = (3, 4)
ANY = pl.BlockSpec(memory_space=pl.ANY)
SMEM = pl.BlockSpec(memory_space=pltpu.SMEM)
VMEM = pl.BlockSpec(memory_space=pltpu.VMEM)
FLOAT = jnp.float32


def columns(amp_ref, slot, source):
    rows = pl.ds(pl.multiple_of(lax.rem(source, 2) * 64, 64), 64)
    return amp_ref[slot, :, rows, :].reshape(1024, 128)


def times(amp, block):
    return lax.dot_general(
        amp, block.reshape(1024, 384), (((0,), (0,)), ((), ())), preferred_element_type=FLOAT
    )


def piece(x, amp_ref, source, block):
    y = x * 4 + source // 2
    return times(
        jnp.concatenate([columns(amp_ref, slot, source) for slot in (y, 7 - y)], axis=1), block[...]
    )


def early_kernel(place, *refs):
    count = len(SHIFTS)
    amps, blocks, (amp, held, out, sems) = refs[:count], refs[count : 2 * count], refs[2 * count :]
    x, y, z, way = place[0], place[1], place[2], 1 - 2 * place[3]
    turns = [lax.rem(way * shift + 8, 8) for shift in SHIFTS]
    copies = [
        pltpu.make_async_copy(ref, amp.at[lax.rem(y + turn, 8)], sems.at[j])
        for j, (ref, turn) in enumerate(zip(amps, turns))
    ] + [
        pltpu.make_async_copy(ref, held.at[lax.rem(z + turn, 8)], sems.at[count + j])
        for j, (ref, turn) in enumerate(zip(blocks, turns))
    ]
    for copy in copies:
        copy.start()
    for turn in LATE:
        amp[lax.rem(y + way * turn + 8, 8)] = jnp.zeros((16, 128, 128), jnp.bfloat16)
    for copy in copies[:count]:
        copy.wait()
    total = None
    for j, turn in enumerate(turns):
        copies[count + j].wait()
        source = lax.rem(z + turn, 8)
        part = piece(x, amp, source, held[source])
        total = part if total is None else total + part
    out[...] = total


def late_sources(place):
    z, way = place[2], 1 - 2 * place[3]
    return [lax.rem(z + way * turn + 8, 8) for turn in LATE]


def middle_kernel(place, early, amp, *refs):
    blocks, out = refs[:-1], refs[-1]
    new = early[...]
    for source, ref in zip(late_sources(place), blocks):
        new = new + piece(place[0], amp, source, ref)
    out[...] = new


def late_kernel(place, middle, held, *refs):
    count = len(LATE)
    amps, blocks, (out, total) = refs[:count], refs[count : 2 * count], refs[2 * count :]
    x, y, way = place[0], place[1], 1 - 2 * place[3]
    sources = late_sources(place)
    total[...] = middle[...]
    for turn, ref in zip(LATE, amps):
        slot = lax.rem(y + way * turn + 8, 8)
        other = jnp.where(slot // 4 == x, 0, 1)
        at = pl.ds(pl.multiple_of(other * 128, 128), 128)
        first = lax.rem(jnp.where(other == 0, slot, 7 - slot), 4) * 2
        for source in (first, first + 1):
            fresh = source != sources[0]
            for late in sources[1:]:
                fresh &= source != late

            @pl.when(fresh)
            def _():
                total[at, :] += times(columns(ref, 0, source), held[source])

            for late, block in zip(sources, blocks):

                @pl.when(source == late)
                def _():
                    total[at, :] += times(columns(ref, 0, source), block[...])

    for n in range(2):
        out[lax.rem(x + n, 2)] = total[n * 128 : (n + 1) * 128].T


def after(block, *arrived):
    return lax.optimization_barrier((block,) + arrived)[0]


def local(integrals, amplitudes, coulomb, row_gap, col_gap):
    place = jnp.stack([lax.axis_index(a) for a in ("xl", "y", "z", "core")])
    place, integrals, amplitudes = lax.optimization_barrier((place, integrals, amplitudes))

    def forth(block, axis, *arrived):
        return lax.ppermute(after(block, *arrived), (axis, "core"), FORTH)

    def back(block, axis, *arrived):
        return lax.ppermute(after(block, *arrived), (axis, "core"), BACK)

    i0 = integrals
    iu1 = forth(i0, "z")
    a0 = lax.ppermute(amplitudes, ("y", "xl"), TRADE)
    id1 = back(i0, "z")
    iu2 = forth(iu1, "z")
    au1 = forth(a0, "y", iu1)
    ad1 = back(a0, "y", iu1)
    id2 = back(id1, "z", a0)
    au2 = forth(au1, "y", id1)
    iu3 = forth(iu2, "z", au1)
    id3 = back(id2, "z", iu2)
    au3 = forth(au2, "y", id2)
    ad2 = back(ad1, "y", au2)
    iu4 = forth(iu3, "z", ad1)
    au4 = forth(au3, "y", iu3)
    ad3 = back(ad2, "y", au3)
    held_shape = jax.ShapeDtypeStruct((8, 16, 64, 384), jnp.bfloat16)
    amp_shape = jax.ShapeDtypeStruct((8, 16, 128, 128), jnp.bfloat16)
    amp, held, early = pl.pallas_call(
        early_kernel,
        out_shape=(amp_shape, held_shape, jax.ShapeDtypeStruct((256, 384), FLOAT)),
        in_specs=[SMEM] + [ANY] * 12,
        out_specs=(VMEM, VMEM, VMEM),
        scratch_shapes=[pltpu.SemaphoreType.DMA((12,))],
        compiler_params=pltpu.CompilerParams(vmem_limit_bytes=24 << 20),
        cost_estimate=pl.CostEstimate(flops=1 << 30, bytes_accessed=16 << 20, transcendentals=0),
    )(place, a0, au1, au2, au3, ad1, ad2, i0, iu1, iu2, iu3, id1, id2)
    middle = pl.pallas_call(
        middle_kernel,
        out_shape=jax.ShapeDtypeStruct((256, 384), FLOAT),
        in_specs=[SMEM] + [VMEM] * 4,
        out_specs=VMEM,
        compiler_params=pltpu.CompilerParams(vmem_limit_bytes=8 << 20),
    )(place, early, amp, id3, iu4)
    shares = pl.pallas_call(
        late_kernel,
        out_shape=jax.ShapeDtypeStruct((2, 384, 128), FLOAT),
        in_specs=[SMEM] + [VMEM] * 6,
        out_specs=VMEM,
        scratch_shapes=[pltpu.VMEM((256, 384), FLOAT)],
        compiler_params=pltpu.CompilerParams(vmem_limit_bytes=8 << 20),
    )(place, middle, held, ad3[None], au4[None], id3, iu4)
    shares = lax.all_to_all(
        shares.reshape(8, 96, 128), ("xl", "xh", "core"), 0, 0, tiled=True
    )
    own = jnp.sum(shares, axis=0)
    gap_sum = row_gap[:, None] + col_gap[None, :]
    return (coulomb.astype(FLOAT) + own) / gap_sum


def solution(mesh):
    fine = Mesh(mesh.devices.reshape(8, 2, 8, 2, 2), ("y", "xl", "z", "xh", "core"))
    layer, col = ("xh", "core"), ("xl", "z")
    placed = (
        P(layer, col, "y"),
        P(layer, "y", col),
        P(("y",) + layer, col),
        P(("y",) + layer),
        P(col),
    )
    return jax.shard_map(
        local, mesh=fine, in_specs=placed, out_specs=P(("y",) + layer, col), check_vma=False
    )
```

```python
import jax
import jax.numpy as jnp
from jax import lax
from jax.experimental import pallas as pl
from jax.experimental.pallas import tpu as pltpu
from jax.sharding import Mesh, PartitionSpec as P

FORTH = [(2 * i + c, 2 * ((i + 1 - 2 * c) % 8) + c) for i in range(8) for c in range(2)]
BACK = [(j, i) for i, j in FORTH]
TRADE = [
    (2 * y + x, 2 * y + x if y // 4 == x else 2 * (7 - y) + 1 - x) for y in range(8) for x in range(2)
]
SHIFTS = (0, -1, -2, -3, 1, 2)
LATE = (3, 4)
ANY = pl.BlockSpec(memory_space=pl.ANY)
SMEM = pl.BlockSpec(memory_space=pltpu.SMEM)
VMEM = pl.BlockSpec(memory_space=pltpu.VMEM)
FLOAT = jnp.float32


def columns(amp_ref, slot, source):
    rows = pl.ds(pl.multiple_of(lax.rem(source, 2) * 64, 64), 64)
    return amp_ref[slot, :, rows, :].reshape(1024, 128)


def times(amp, block):
    return lax.dot_general(
        amp, block.reshape(1024, 384), (((0,), (0,)), ((), ())), preferred_element_type=FLOAT
    )


def piece(x, amp_ref, source, block):
    y = x * 4 + source // 2
    return times(
        jnp.concatenate([columns(amp_ref, slot, source) for slot in (y, 7 - y)], axis=1), block[...]
    )


def early_kernel(place, *refs):
    count = len(SHIFTS)
    amps, blocks, (amp, held, out, sems) = refs[:count], refs[count : 2 * count], refs[2 * count :]
    x, y, z, way = place[0], place[1], place[2], 1 - 2 * place[3]
    turns = [lax.rem(way * shift + 8, 8) for shift in SHIFTS]
    copies = [
        pltpu.make_async_copy(ref, amp.at[lax.rem(y + turn, 8)], sems.at[j])
        for j, (ref, turn) in enumerate(zip(amps, turns))
    ] + [
        pltpu.make_async_copy(ref, held.at[lax.rem(z + turn, 8)], sems.at[count + j])
        for j, (ref, turn) in enumerate(zip(blocks, turns))
    ]
    for copy in copies:
        copy.start()
    for turn in LATE:
        amp[lax.rem(y + way * turn + 8, 8)] = jnp.zeros((16, 128, 128), jnp.bfloat16)
    for copy in copies[:count]:
        copy.wait()
    total = None
    for j, turn in enumerate(turns):
        copies[count + j].wait()
        source = lax.rem(z + turn, 8)
        part = piece(x, amp, source, held[source])
        total = part if total is None else total + part
    out[...] = total


def late_sources(place):
    z, way = place[2], 1 - 2 * place[3]
    return [lax.rem(z + way * turn + 8, 8) for turn in LATE]


def middle_kernel(place, early, amp, *refs):
    blocks, out = refs[:-1], refs[-1]
    new = early[...]
    for source, ref in zip(late_sources(place), blocks):
        new = new + piece(place[0], amp, source, ref)
    out[...] = new


def add_late(turn, place, total, amp, held, blocks):
    x, y, way = place[0], place[1], 1 - 2 * place[3]
    sources = late_sources(place)
    slot = lax.rem(y + way * turn + 8, 8)
    other = jnp.where(slot // 4 == x, 0, 1)
    at = pl.ds(pl.multiple_of(other * 128, 128), 128)
    first = lax.rem(jnp.where(other == 0, slot, 7 - slot), 4) * 2
    for source in (first, first + 1):
        fresh = source != sources[0]
        for late in sources[1:]:
            fresh &= source != late

        @pl.when(fresh)
        def _():
            total[at, :] += times(columns(amp, 0, source), held[source])

        for late, block in zip(sources, blocks):

            @pl.when(source == late)
            def _():
                total[at, :] += times(columns(amp, 0, source), block[...])


def third_kernel(place, middle, held, amp, low, high, total):
    total[...] = middle[...]
    add_late(LATE[0], place, total, amp, held, (low, high))


def late_kernel(place, third, held, amp, low, high, out, total):
    total[...] = third[...]
    add_late(LATE[1], place, total, amp, held, (low, high))
    for n in range(2):
        out[lax.rem(place[0] + n, 2)] = total[n * 128 : (n + 1) * 128].T


def after(block, *arrived):
    return lax.optimization_barrier((block,) + arrived)[0]


def local(integrals, amplitudes, coulomb, row_gap, col_gap):
    place = jnp.stack([lax.axis_index(a) for a in ("xl", "y", "z", "core")])
    place, integrals, amplitudes = lax.optimization_barrier((place, integrals, amplitudes))

    def forth(block, axis, *arrived):
        return lax.ppermute(after(block, *arrived), (axis, "core"), FORTH)

    def back(block, axis, *arrived):
        return lax.ppermute(after(block, *arrived), (axis, "core"), BACK)

    i0 = integrals
    iu1 = forth(i0, "z")
    a0 = lax.ppermute(amplitudes, ("y", "xl"), TRADE)
    id1 = back(i0, "z")
    iu2 = forth(iu1, "z")
    au1 = forth(a0, "y", iu1)
    ad1 = back(a0, "y", iu1)
    id2 = back(id1, "z", a0)
    au2 = forth(au1, "y", id1)
    iu3 = forth(iu2, "z", au1)
    id3 = back(id2, "z", iu2)
    au3 = forth(au2, "y", id2)
    ad2 = back(ad1, "y", au2)
    iu4 = forth(iu3, "z", ad1)
    au4 = forth(au3, "y", iu3)
    ad3 = back(ad2, "y", au3)
    held_shape = jax.ShapeDtypeStruct((8, 16, 64, 384), jnp.bfloat16)
    amp_shape = jax.ShapeDtypeStruct((8, 16, 128, 128), jnp.bfloat16)
    amp, held, early = pl.pallas_call(
        early_kernel,
        out_shape=(amp_shape, held_shape, jax.ShapeDtypeStruct((256, 384), FLOAT)),
        in_specs=[SMEM] + [ANY] * 12,
        out_specs=(VMEM, VMEM, VMEM),
        scratch_shapes=[pltpu.SemaphoreType.DMA((12,))],
        compiler_params=pltpu.CompilerParams(vmem_limit_bytes=24 << 20),
        cost_estimate=pl.CostEstimate(flops=1 << 30, bytes_accessed=16 << 20, transcendentals=0),
    )(place, a0, au1, au2, au3, ad1, ad2, i0, iu1, iu2, iu3, id1, id2)
    middle = pl.pallas_call(
        middle_kernel,
        out_shape=jax.ShapeDtypeStruct((256, 384), FLOAT),
        in_specs=[SMEM] + [VMEM] * 4,
        out_specs=VMEM,
        compiler_params=pltpu.CompilerParams(vmem_limit_bytes=8 << 20),
    )(place, early, amp, id3, iu4)
    third = pl.pallas_call(
        third_kernel,
        out_shape=jax.ShapeDtypeStruct((256, 384), FLOAT),
        in_specs=[SMEM] + [VMEM] * 5,
        out_specs=VMEM,
        compiler_params=pltpu.CompilerParams(vmem_limit_bytes=8 << 20),
    )(place, middle, held, ad3[None], id3, iu4)
    shares = pl.pallas_call(
        late_kernel,
        out_shape=jax.ShapeDtypeStruct((2, 384, 128), FLOAT),
        in_specs=[SMEM] + [VMEM] * 5,
        out_specs=VMEM,
        scratch_shapes=[pltpu.VMEM((256, 384), FLOAT)],
        compiler_params=pltpu.CompilerParams(vmem_limit_bytes=8 << 20),
    )(place, third, held, au4[None], id3, iu4)
    shares = lax.all_to_all(
        shares.reshape(8, 96, 128), ("xl", "xh", "core"), 0, 0, tiled=True
    )
    own = jnp.sum(shares, axis=0)
    gap_sum = row_gap[:, None] + col_gap[None, :]
    return (coulomb.astype(FLOAT) + own) / gap_sum


def solution(mesh):
    fine = Mesh(mesh.devices.reshape(8, 2, 8, 2, 2), ("y", "xl", "z", "xh", "core"))
    layer, col = ("xh", "core"), ("xl", "z")
    placed = (
        P(layer, col, "y"),
        P(layer, "y", col),
        P(("y",) + layer, col),
        P(("y",) + layer),
        P(col),
    )
    return jax.shard_map(
        local, mesh=fine, in_specs=placed, out_specs=P(("y",) + layer, col), check_vma=False
    )
```

```python
import jax
import jax.numpy as jnp
from jax import lax
from jax.experimental import pallas as pl
from jax.experimental.pallas import tpu as pltpu
from jax.sharding import Mesh, PartitionSpec as P

FORTH = [(2 * i + c, 2 * ((i + 1 - 2 * c) % 8) + c) for i in range(8) for c in range(2)]
BACK = [(j, i) for i, j in FORTH]
TRADE = [
    (2 * y + x, 2 * y + x if y // 4 == x else 2 * (7 - y) + 1 - x) for y in range(8) for x in range(2)
]
SHIFTS = (0, -1, -2, -3, 1, 2)
LATE = (3, 4)
ANY = pl.BlockSpec(memory_space=pl.ANY)
SMEM = pl.BlockSpec(memory_space=pltpu.SMEM)
VMEM = pl.BlockSpec(memory_space=pltpu.VMEM)
FLOAT = jnp.float32


def columns(amp_ref, slot, source):
    rows = pl.ds(pl.multiple_of(lax.rem(source, 2) * 64, 64), 64)
    return amp_ref[slot, :, rows, :].reshape(1024, 128)


def times(amp, block):
    return lax.dot_general(
        amp, block.reshape(1024, 384), (((0,), (0,)), ((), ())), preferred_element_type=FLOAT
    )


def piece(x, amp_ref, source, block):
    y = x * 4 + source // 2
    return times(
        jnp.concatenate([columns(amp_ref, slot, source) for slot in (y, 7 - y)], axis=1), block[...]
    )


def early_kernel(place, *refs):
    count = len(SHIFTS)
    amps, blocks, (amp, held, out, sems) = refs[:count], refs[count : 2 * count], refs[2 * count :]
    x, y, z, way = place[0], place[1], place[2], 1 - 2 * place[3]
    turns = [lax.rem(way * shift + 8, 8) for shift in SHIFTS]
    copies = [
        pltpu.make_async_copy(ref, amp.at[lax.rem(y + turn, 8)], sems.at[j])
        for j, (ref, turn) in enumerate(zip(amps, turns))
    ] + [
        pltpu.make_async_copy(ref, held.at[lax.rem(z + turn, 8)], sems.at[count + j])
        for j, (ref, turn) in enumerate(zip(blocks, turns))
    ]
    for copy in copies:
        copy.start()
    for turn in LATE:
        amp[lax.rem(y + way * turn + 8, 8)] = jnp.zeros((16, 128, 128), jnp.bfloat16)
    for copy in copies[:count]:
        copy.wait()
    total = None
    for j, turn in enumerate(turns):
        part = piece(x, amp, lax.rem(z + turn, 8), blocks[j])
        total = part if total is None else total + part
    out[...] = total
    for copy in copies[count:]:
        copy.wait()


def late_sources(place):
    z, way = place[2], 1 - 2 * place[3]
    return [lax.rem(z + way * turn + 8, 8) for turn in LATE]


def middle_kernel(place, early, amp, *refs):
    blocks, out = refs[:-1], refs[-1]
    new = early[...]
    for source, ref in zip(late_sources(place), blocks):
        new = new + piece(place[0], amp, source, ref)
    out[...] = new


def add_late(turn, place, total, amp, held, blocks):
    x, y, way = place[0], place[1], 1 - 2 * place[3]
    sources = late_sources(place)
    slot = lax.rem(y + way * turn + 8, 8)
    other = jnp.where(slot // 4 == x, 0, 1)
    at = pl.ds(pl.multiple_of(other * 128, 128), 128)
    first = lax.rem(jnp.where(other == 0, slot, 7 - slot), 4) * 2
    for source in (first, first + 1):
        fresh = source != sources[0]
        for late in sources[1:]:
            fresh &= source != late

        @pl.when(fresh)
        def _():
            total[at, :] += times(columns(amp, 0, source), held[source])

        for late, block in zip(sources, blocks):

            @pl.when(source == late)
            def _():
                total[at, :] += times(columns(amp, 0, source), block[...])


def third_kernel(place, middle, held, amp, low, high, total):
    total[...] = middle[...]
    add_late(LATE[0], place, total, amp, held, (low, high))


def late_kernel(place, third, held, amp, low, high, out, total):
    total[...] = third[...]
    add_late(LATE[1], place, total, amp, held, (low, high))
    for n in range(2):
        out[lax.rem(place[0] + n, 2)] = total[n * 128 : (n + 1) * 128].T


def after(block, *arrived):
    return lax.optimization_barrier((block,) + arrived)[0]


def local(integrals, amplitudes, coulomb, row_gap, col_gap):
    place = jnp.stack([lax.axis_index(a) for a in ("xl", "y", "z", "core")])
    place, integrals, amplitudes = lax.optimization_barrier((place, integrals, amplitudes))

    def forth(block, axis, *arrived):
        return lax.ppermute(after(block, *arrived), (axis, "core"), FORTH)

    def back(block, axis, *arrived):
        return lax.ppermute(after(block, *arrived), (axis, "core"), BACK)

    i0 = integrals
    iu1 = forth(i0, "z")
    a0 = lax.ppermute(amplitudes, ("y", "xl"), TRADE)
    id1 = back(i0, "z")
    iu2 = forth(iu1, "z")
    au1 = forth(a0, "y", iu1)
    ad1 = back(a0, "y", iu1)
    id2 = back(id1, "z", a0)
    au2 = forth(au1, "y", id1)
    iu3 = forth(iu2, "z", au1)
    id3 = back(id2, "z", iu2)
    au3 = forth(au2, "y", id2)
    ad2 = back(ad1, "y", au2)
    iu4 = forth(iu3, "z", ad1)
    au4 = forth(au3, "y", iu3)
    ad3 = back(ad2, "y", au3)
    held_shape = jax.ShapeDtypeStruct((8, 16, 64, 384), jnp.bfloat16)
    amp_shape = jax.ShapeDtypeStruct((8, 16, 128, 128), jnp.bfloat16)
    amp, held, early = pl.pallas_call(
        early_kernel,
        out_shape=(amp_shape, held_shape, jax.ShapeDtypeStruct((256, 384), FLOAT)),
        in_specs=[SMEM] + [ANY] * 6 + [VMEM] * 6,
        out_specs=(VMEM, VMEM, VMEM),
        scratch_shapes=[pltpu.SemaphoreType.DMA((12,))],
        compiler_params=pltpu.CompilerParams(vmem_limit_bytes=24 << 20),
        cost_estimate=pl.CostEstimate(flops=1 << 30, bytes_accessed=16 << 20, transcendentals=0),
    )(place, a0, au1, au2, au3, ad1, ad2, i0, iu1, iu2, iu3, id1, id2)
    middle = pl.pallas_call(
        middle_kernel,
        out_shape=jax.ShapeDtypeStruct((256, 384), FLOAT),
        in_specs=[SMEM] + [VMEM] * 4,
        out_specs=VMEM,
        compiler_params=pltpu.CompilerParams(vmem_limit_bytes=8 << 20),
    )(place, early, amp, id3, iu4)
    third = pl.pallas_call(
        third_kernel,
        out_shape=jax.ShapeDtypeStruct((256, 384), FLOAT),
        in_specs=[SMEM] + [VMEM] * 5,
        out_specs=VMEM,
        compiler_params=pltpu.CompilerParams(vmem_limit_bytes=8 << 20),
    )(place, middle, held, ad3[None], id3, iu4)
    shares = pl.pallas_call(
        late_kernel,
        out_shape=jax.ShapeDtypeStruct((2, 384, 128), FLOAT),
        in_specs=[SMEM] + [VMEM] * 5,
        out_specs=VMEM,
        scratch_shapes=[pltpu.VMEM((256, 384), FLOAT)],
        compiler_params=pltpu.CompilerParams(vmem_limit_bytes=8 << 20),
    )(place, third, held, au4[None], id3, iu4)
    shares = lax.all_to_all(
        shares.reshape(8, 96, 128), ("xl", "xh", "core"), 0, 0, tiled=True
    )
    own = jnp.sum(shares, axis=0)
    gap_sum = row_gap[:, None] + col_gap[None, :]
    return (coulomb.astype(FLOAT) + own) / gap_sum


def solution(mesh):
    fine = Mesh(mesh.devices.reshape(8, 2, 8, 2, 2), ("y", "xl", "z", "xh", "core"))
    layer, col = ("xh", "core"), ("xl", "z")
    placed = (
        P(layer, col, "y"),
        P(layer, "y", col),
        P(("y",) + layer, col),
        P(("y",) + layer),
        P(col),
    )
    return jax.shard_map(
        local, mesh=fine, in_specs=placed, out_specs=P(("y",) + layer, col), check_vma=False
    )
```
